32 devices in a mesh: group: 8 (over y, x, core), leaf: 4 (over z).
Axes of the slice: x: 2, y: 2, z: 4, core: 2. Of those that a mesh axis runs over, the one named last changes fastest.
Arguments:
- leaf_mass: bfloat16 [32, 512, 512], P(('group', 'leaf')), may hold values from -23 to 23, as said below
- leaf_damp: bfloat16 [32, 512, 512], P(('group', 'leaf')), may hold values from -12 to 12, as said below
- mass_coupling: bfloat16 [32, 512, 1536], P(('group', 'leaf')), may hold values from -6 to 6
- damp_coupling: bfloat16 [32, 512, 1536], P(('group', 'leaf')), may hold values from -6 to 6
- leaf_modes: bfloat16 [32, 512, 1536], P(('group', 'leaf')), may hold values from -0.15625 to 0.15625
- interface_blocks: int32 [32, 12], P(('group', 'leaf')), may hold values from 0 to 11, each once within a row
- mid_modes: bfloat16 [8, 1536, 256], P('group', 'leaf'), may hold values from -0.15625 to 0.15625
- mid_constraint: bfloat16 [8, 1536, 1024], P('group', 'leaf'), may hold values from -0.109375 to 0.109375
Outputs:
- coupling_mass: float32 [32, 512, 256], P(('group', 'leaf'))
- coupling_damp: float32 [32, 512, 256], P(('group', 'leaf'))
- modal_mass: float32 [8, 256, 1280], P('group', 'leaf')
- modal_damp: float32 [8, 256, 1280], P('group', 'leaf')
- root_mass: float32 [1024, 1024], P(('group', 'leaf'))
- root_damp: float32 [1024, 1024], P(('group', 'leaf'))
The draws below stay inside these ranges and needn't reach their ends.
Inputs may be any that keep to these rules, and one draw needn't show every extreme that they name: `interface_blocks`: each row is a permutation of 0 to 11. `leaf_mass`: each leaf's block is symmetric. `leaf_damp`: each leaf's block is symmetric.
All inputs are finite; a program needn't handle non-finite values.
Results may differ from the reference program's by a relative error of at most 0.0049.
Values may be sent and summed in bfloat16 or wider, within the bound.
A program may use at most 128 MiB of HBM per device.

```python
import jax
import jax.numpy as jnp
from jax import lax

LO = 512
SEP = 1536
MODES = 256
ROOT = 1024
BLK = 128
NBLK = 12
LEAVES = 32
N_GROUP = 8
N_LEAF = 4


def symmetric_block(key, factor):
    base = jnp.clip(jax.random.normal(key, (LEAVES, LO, LO), jnp.float32), -4.0, 4.0)
    return ((base + jnp.swapaxes(base, 1, 2)) * factor).astype(jnp.bfloat16)


def draw_leaf_mass(key, part):
    return symmetric_block(jax.random.fold_in(key, 11), 2.83)


def draw_leaf_damp(key, part):
    return symmetric_block(jax.random.fold_in(key, 23), 1.4)


def with_spikes(result, stream_key, source, target, blocks, factor):
    def block_of(axis_at):
        return (jnp.arange(result.shape[axis_at]) // (result.shape[axis_at] // blocks)).reshape((-1,) + (1,) * (result.ndim - 1 - axis_at))

    one_side = jax.random.permutation(stream_key, blocks)[block_of(target)]
    other_side = (block_of(target) + blocks // 2) % blocks
    return jnp.where((block_of(source) == one_side) | (block_of(source) == other_side), factor * result, result)


def steps_of(stream_key, shape, pieces, smallest, high):
    loudness, own = 1.0, jax.random.fold_in(stream_key, 6)
    for axis_at, parts in pieces:
        steps = jnp.exp(jax.random.uniform(jax.random.fold_in(own, axis_at), (parts,), jnp.float32, smallest / len(pieces), high / len(pieces)))
        loudness = loudness * jnp.repeat(steps, shape[axis_at] // parts).reshape([-1 if axis == axis_at else 1 for axis in range(len(shape))])
    return loudness


def scatter_about(rng, dims, width, most, pieces=(), kind=jnp.bfloat16):
    values = width * jax.random.normal(rng, dims, jnp.float32)
    if pieces:
        values = values * steps_of(rng, dims, pieces, -0.22, 0.18)
    return jnp.clip(values, -most, most).astype(kind)


def gaussian_with(rng, extent, width, limit, shards, heavy, kind=jnp.bfloat16):
    array = width * jax.random.normal(rng, extent, jnp.float32)
    if shards:
        array = array * steps_of(rng, extent, shards, -0.22, 0.18)
    return jnp.clip(with_spikes(array, jax.random.fold_in(rng, 3), *heavy), -limit, limit).astype(kind)


def setup_inputs(seed: int = 0) -> dict:
    seeds = jax.random.split(jax.random.key(seed), 9)
    return {
        "leaf_mass": draw_leaf_mass(jax.random.fold_in(seeds[8], 71), 0),
        "leaf_damp": draw_leaf_damp(jax.random.fold_in(seeds[8], 71), 0),
        "mass_coupling": scatter_about(seeds[2], (LEAVES, LO, SEP), 1.0, 6.0, ((0, 32),)),
        "damp_coupling": scatter_about(seeds[3], (LEAVES, LO, SEP), 1.0, 6.0, ((0, 32),)),
        "leaf_modes": scatter_about(seeds[4], (LEAVES, LO, SEP), 0.01, 0.15625, ((0, 32),)),
        "interface_blocks": jax.vmap(lambda own: jax.random.permutation(own, NBLK))(jax.random.split(seeds[5], LEAVES)).reshape((LEAVES, NBLK)).astype(jnp.int32),
        "mid_modes": scatter_about(seeds[6], (N_GROUP, SEP, MODES), SEP ** -0.5, 0.15625, ((0, 8), (1, 4))),
        "mid_constraint": gaussian_with(seeds[7], (N_GROUP, SEP, ROOT), (SEP * 4) ** -0.5, 0.109375, ((0, 8), (1, 4)), (1, 2, 4, 2.0)),
    }


def to_middle(matrix, inverse):
    return matrix.reshape(LO, NBLK, BLK)[:, inverse, :].reshape(LO, SEP)


def reference(leaf_mass, leaf_damp, mass_coupling, damp_coupling, leaf_modes, interface_blocks, mid_modes, mid_constraint):
    def one_group(group_id):
        eigen_modes = lax.dynamic_index_in_dim(mid_modes, group_id, 0, keepdims=False)
        root_shapes = lax.dynamic_index_in_dim(mid_constraint, group_id, 0, keepdims=False)
        mode_basis = jnp.concatenate([eigen_modes, root_shapes], axis=1)

        def one_leaf(totals, member):
            leaf_id = group_id * N_LEAF + member

            def select(stacked):
                return lax.dynamic_index_in_dim(stacked, leaf_id, 0, keepdims=False)

            inverse = jnp.argsort(select(interface_blocks)).astype(jnp.int32)
            constraint = to_middle(select(leaf_modes), inverse)
            left = jnp.dot(constraint, mode_basis, preferred_element_type=jnp.float32).astype(jnp.bfloat16)
            new_totals = []
            couplings = []
            pairs = ((select(leaf_mass), select(mass_coupling)), (select(leaf_damp), select(damp_coupling)))
            for index in range(2):
                leaf_block, side_block = pairs[index]
                side_middle = to_middle(side_block, inverse).astype(jnp.float32)
                product = jnp.dot(leaf_block, constraint, preferred_element_type=jnp.float32)
                half_work = (0.5 * product + side_middle).astype(jnp.bfloat16)
                full_work = (product + side_middle).astype(jnp.bfloat16)
                right = jnp.dot(half_work, mode_basis, preferred_element_type=jnp.float32).astype(jnp.bfloat16)
                folded = jnp.dot(left.T, right, preferred_element_type=jnp.float32)
                projected = folded + folded.T
                couplings.append(jnp.dot(full_work, eigen_modes, preferred_element_type=jnp.float32))
                new_totals.append(totals[2 * index] + projected[:MODES])
                new_totals.append(totals[2 * index + 1] + projected[MODES:, MODES:])
            return tuple(new_totals), (couplings[0], couplings[1])

        modal_zero = jnp.zeros((MODES, MODES + ROOT), jnp.float32)
        root_zero = jnp.zeros((ROOT, ROOT), jnp.float32)
        sums, couplings = lax.scan(one_leaf, (modal_zero, root_zero, modal_zero, root_zero), jnp.arange(N_LEAF, dtype=jnp.int32))
        return couplings[0], couplings[1], sums[0], sums[2], sums[1], sums[3]

    def add_group(carry, group_id):
        outs = one_group(group_id)
        return (carry[0] + outs[4], carry[1] + outs[5]), (outs[0], outs[1], outs[2], outs[3])

    root_zero = jnp.zeros((ROOT, ROOT), jnp.float32)
    roots, stacks = lax.scan(add_group, (root_zero, root_zero), jnp.arange(N_GROUP, dtype=jnp.int32))
    coupling_mass = stacks[0].reshape(LEAVES, LO, MODES)
    coupling_damp = stacks[1].reshape(LEAVES, LO, MODES)
    return (coupling_mass, coupling_damp, stacks[2], stacks[3], roots[0], roots[1])
```

```python
import jax
import jax.numpy as jnp
from jax import lax
from jax.experimental import pallas as pl
from jax.experimental.pallas import tpu as pltpu
from jax.sharding import PartitionSpec as P


def to_middle(stacked, onehot, block_count, block_size):
    rows_total, width_total = stacked.shape
    moved = jnp.einsum(
        "lbk,bj->ljk",
        stacked.reshape(rows_total, block_count, block_size),
        onehot,
        preferred_element_type=jnp.float32,
    )
    return moved.astype(jnp.bfloat16).reshape(rows_total, width_total)


def left_product(first_operand, second_operand):
    return lax.dot_general(
        first_operand, second_operand, (((0,), (0,)), ((), ())), preferred_element_type=jnp.float32
    )


def body(
    leaf_mass,
    leaf_damp,
    mass_coupling,
    damp_coupling,
    leaf_modes,
    interface_blocks,
    mid_modes,
    mid_constraint,
):
    leaf_order = leaf_mass.shape[1]
    block_count = interface_blocks.shape[1]
    sep_width = leaf_modes.shape[2]
    block_size = sep_width // block_count
    mode_count = mid_modes.shape[2]
    root_width = mid_constraint.shape[2]
    basis_width = mode_count + root_width
    leaf_count = lax.axis_size("leaf")
    group_count = lax.axis_size("group")
    onehot = (
        interface_blocks[0][:, None] == jnp.arange(block_count, dtype=jnp.int32)[None, :]
    ).astype(jnp.bfloat16)
    placed = to_middle(
        jnp.concatenate([leaf_modes[0], mass_coupling[0], damp_coupling[0]], axis=0),
        onehot,
        block_count,
        block_size,
    )
    constraint = placed[:leaf_order]
    sides = placed[leaf_order:].astype(jnp.float32)
    product = jnp.dot(
        jnp.concatenate([leaf_mass[0], leaf_damp[0]], axis=0),
        constraint,
        preferred_element_type=jnp.float32,
    )
    half_work = (0.5 * product + sides).astype(jnp.bfloat16)
    full_work = (product + sides).astype(jnp.bfloat16)
    basis_rows = jnp.concatenate([mid_modes[0], mid_constraint[0]], axis=1)
    mode_basis = lax.all_gather(basis_rows, "leaf", axis=0, tiled=True)
    left_sum = jnp.dot(constraint, mode_basis, preferred_element_type=jnp.float32)
    right_sum = jnp.dot(half_work, mode_basis, preferred_element_type=jnp.float32)
    coupling = jnp.dot(full_work, mode_basis[:, :mode_count], preferred_element_type=jnp.float32)
    left_part = left_sum.astype(jnp.bfloat16)
    right_part = right_sum.astype(jnp.bfloat16)
    right_mass = right_part[:leaf_order]
    right_damp = right_part[leaf_order:]

    def projected_rows(first_row, amount, first_col):
        left_rows = lax.dynamic_slice_in_dim(left_part, first_row, amount, 1)
        right_rows = lax.dynamic_slice_in_dim(right_part, first_row, amount, 1)
        left_cols = left_part[:, first_col:]
        mass_term = left_product(left_rows, right_mass[:, first_col:]) + left_product(
            right_rows[:leaf_order], left_cols
        )
        damp_term = left_product(left_rows, right_damp[:, first_col:]) + left_product(
            right_rows[leaf_order:], left_cols
        )
        return jnp.concatenate([mass_term, damp_term], axis=1)

    modal_part = lax.psum_scatter(
        projected_rows(jnp.int32(0), mode_count // leaf_count * lax.axis_size("leaf"), 0),
        "leaf",
        scatter_dimension=0,
        tiled=True,
    )
    root_part = lax.psum_scatter(
        projected_rows(
            jnp.int32(0) + mode_count,
            root_width // (group_count * leaf_count) * lax.axis_size(("group", "leaf")),
            mode_count,
        ),
        ("group", "leaf"),
        scatter_dimension=0,
        tiled=True,
    )
    return (
        coupling[:leaf_order][None],
        coupling[leaf_order:][None],
        modal_part[:, :basis_width][None],
        modal_part[:, basis_width:][None],
        root_part[:, :root_width],
        root_part[:, root_width:],
    )


F32 = jnp.float32
BF16 = jnp.bfloat16
MESH = pl.DeviceIdType.MESH
STRIP = 128
TILE = 256


def fused_kernel(
    leaf_mass, leaf_damp, mass_side, damp_side, leaf_modes, blocks, mid_modes, mid_constraint,
    coup_mass, coup_damp, modal_mass, modal_damp, root_mass, root_damp,
    mass_v, damp_v, mside_v, dside_v, modes_v,
    part0, part1, part2, work, full, q_one, q_two,
    root_part, recv_a, recv_b, recv_c, root_strip, recv_d, modal_part, recv_m,
    in_sem, own_sem, gs_sem, gr_sem, as_sem, ar_sem, bs_sem, br_sem, cs_sem, cr_sem,
    ds_sem, dr_sem, ms_sem, mr_sem,
):
    group = lax.axis_index("group")
    leaf = lax.axis_index("leaf")
    leaves = lax.axis_size("leaf")
    core, col, row = lax.rem(group, 2), lax.rem(group // 2, 2), group // 4
    by_core = (group + 1 - 2 * core, leaf)
    by_x = (group + 2 - 4 * col, leaf)
    by_y = (group + 4 - 8 * row, leaf)
    order = mass_v.shape[0]
    modes = mid_modes.shape[2]
    root = mid_constraint.shape[2]
    shard = mid_modes.shape[1]
    half = root // 2
    strip_rows = root // 8
    out_rows = root_mass.shape[0]
    modal_rows = modal_mass.shape[1]
    width = modes + root
    others = [(group, lax.rem(leaf + d, leaves)) for d in range(1, 4)]

    inputs = [
        pltpu.make_async_copy(a.at[0], b, in_sem.at[i])
        for i, (a, b) in enumerate(
            ((leaf_mass, mass_v), (leaf_damp, damp_v), (mass_side, mside_v), (damp_side, dside_v), (leaf_modes, modes_v))
        )
    ]
    own_src = (mid_constraint.at[0, :, 0:half], mid_constraint.at[0, :, half:root], mid_modes.at[0])
    parts = (part0, part1, part2)

    def rows_of(index):
        return pl.ds(pl.multiple_of(index * shard, shard), shard)

    own = [
        pltpu.make_async_copy(own_src[p], parts[p].at[rows_of(leaf), :], own_sem.at[p]) for p in range(3)
    ]

    barrier = pltpu.get_barrier_semaphore()
    for dev in [by_core, by_x, by_y] + others:
        pl.semaphore_signal(barrier, inc=1, device_id=dev, device_id_type=MESH)
    for c in inputs:
        c.start()
    for c in own:
        c.start()
    pl.semaphore_wait(barrier, 6)

    def hop(p, way, t):
        index = leaf - t if way == 0 else leaf + t
        target = leaf + 1 if way == 0 else leaf - 1
        place = parts[p].at[rows_of(index), :]
        return pltpu.make_async_remote_copy(
            src_ref=own_src[p] if t == 0 else place,
            dst_ref=place,
            send_sem=gs_sem.at[p, way, t],
            recv_sem=gr_sem.at[p, way, t],
            device_id=(group, target),
            device_id_type=MESH,
        )

    def sends(way, t):
        if way == 0:
            return (leaf + 1 < leaves) & (leaf >= t)
        return (leaf >= 1) & (leaf + t < leaves)

    def start_hop(p, t):
        for way in range(2):
            @pl.when(sends(way, t))
            def _():
                hop(p, way, t).start()

    def arrive(p, t):
        for way in range(2):
            has = leaf >= t if way == 0 else leaf + t < leaves

            @pl.when(has)
            def _():
                index = leaf - t if way == 0 else leaf + t
                pltpu.make_async_remote_copy(
                    src_ref=parts[p].at[rows_of(index), :],
                    dst_ref=parts[p].at[rows_of(index), :],
                    send_sem=gs_sem.at[p, way, t],
                    recv_sem=gr_sem.at[p, way, t - 1],
                    device_id=(group, lax.rem(leaf + 1, leaves)),
                    device_id_type=MESH,
                ).wait_recv()
        if t < 3:
            start_hop(p, t)

    start_hop(0, 0)
    for c in inputs:
        c.wait()

    @pl.loop(0, 6)
    def _(pair):
        chosen = [blocks[2 * pair + i].astype(BF16) for i in range(2)]

        def moved(ref):
            sums = [None, None]
            for b in range(12):
                lanes = slice(128 * b, 128 * (b + 1))
                for i in range(2):
                    term = ref[:, lanes] * chosen[i][:, lanes]
                    sums[i] = term if b == 0 else sums[i] + term
            return jnp.concatenate(sums, axis=1)

        here = pl.ds(pl.multiple_of(pair * 256, 256), 256)
        constraint = moved(modes_v)
        work[order:2 * order, here] = constraint
        for k, (block, side) in enumerate(((mass_v, mside_v), (damp_v, dside_v))):
            product = jnp.dot(block[...], constraint, preferred_element_type=F32)
            side_part = moved(side).astype(F32)
            work[2 * order * k:2 * order * k + order, here] = (0.5 * product + side_part).astype(BF16)
            full[order * k:order * (k + 1), here] = (product + side_part).astype(BF16)

    def multiply(p, first, size):
        @pl.loop(0, 6)
        def _(m):
            tile = work[pl.ds(pl.multiple_of(m * TILE, TILE), TILE), :]
            value = jnp.dot(tile, parts[p][...], preferred_element_type=F32).astype(BF16)
            other = 4 - 2 * (m // 2) + lax.rem(m, 2)
            q_one[pl.ds(pl.multiple_of(m * TILE, TILE), TILE), first:first + size] = value
            q_two[pl.ds(pl.multiple_of(other * TILE, TILE), TILE), first:first + size] = value

    def pairs_of(k):
        if k == 0:
            return q_two, q_one
        return q_one, q_two

    own[0].wait()
    for t in range(1, 4):
        arrive(0, t)
        if t == 2:
            start_hop(1, 0)
    multiply(0, modes, half)
    own[1].wait()
    for t in range(1, 4):
        arrive(1, t)
        if t == 2:
            start_hop(2, 0)
    multiply(1, modes + half, half)
    arrive(2, 1)

    def strip_value(s, k):
        turned, straight = pairs_of(k)
        columns = pl.ds(pl.multiple_of(modes + s * strip_rows, 128), strip_rows)
        lhs = turned[order:3 * order, columns]
        return lax.dot_general(
            lhs, straight[0:2 * order, modes:width], (((0,), (0,)), ((), ())), preferred_element_type=F32
        )

    def fill_strip(s):
        for k in range(2):
            root_part[s, :, k * root:(k + 1) * root] = strip_value(s, k).astype(BF16)

    chips = (
        2 * (1 - row) + 1 - col,
        2 * row + 1 - col,
        2 * (1 - row) + col,
        2 * row + col,
    )

    def copy_a(i):
        return pltpu.make_async_remote_copy(
            src_ref=root_part.at[2 * chips[i] + 1 - core],
            dst_ref=recv_a.at[i],
            send_sem=as_sem.at[i],
            recv_sem=ar_sem.at[i],
            device_id=by_core,
            device_id_type=MESH,
        )

    def copy_b(k, slot, device):
        chip = chips[0] if slot == 0 else chips[1 + k]
        return pltpu.make_async_remote_copy(
            src_ref=root_part.at[2 * chip + core, :, k * root:(k + 1) * root],
            dst_ref=recv_b.at[k, slot],
            send_sem=bs_sem.at[k, slot],
            recv_sem=br_sem.at[k, slot],
            device_id=device,
            device_id_type=MESH,
        )

    def copy_c(k, device):
        chip = chips[2 - k]
        return pltpu.make_async_remote_copy(
            src_ref=root_part.at[2 * chip + core, :, k * root:(k + 1) * root],
            dst_ref=recv_c.at[k],
            send_sem=cs_sem.at[k],
            recv_sem=cr_sem.at[k],
            device_id=device,
            device_id_type=MESH,
        )

    for i in range(4):
        fill_strip(2 * chips[i] + 1 - core)
        copy_a(i).start()
    arrive(2, 2)
    for i in range(4):
        s = 2 * chips[i] + core
        fill_strip(s)
        copy_a(i).wait_recv()
        root_part[s] = (root_part[s].astype(F32) + recv_a[i].astype(F32)).astype(BF16)
        if i == 0:
            copy_b(0, 0, by_x).start()
            copy_b(1, 0, by_y).start()
        if i == 1:
            copy_b(0, 1, by_x).start()
        if i == 2:
            copy_b(1, 1, by_y).start()
    own[2].wait()
    arrive(2, 3)
    multiply(2, 0, modes)

    def copy_m(k, d):
        target = lax.rem(leaf + d, leaves)
        return pltpu.make_async_remote_copy(
            src_ref=modal_part.at[k, pl.ds(pl.multiple_of(target * modal_rows, modal_rows), modal_rows), :],
            dst_ref=recv_m.at[k, d - 1],
            send_sem=ms_sem.at[k, d - 1],
            recv_sem=mr_sem.at[k, d - 1],
            device_id=(group, target),
            device_id_type=MESH,
        )

    for k in range(2):
        turned, straight = pairs_of(k)
        modal_part[k] = lax.dot_general(
            turned[order:3 * order, 0:modes], straight[0:2 * order, :], (((0,), (0,)), ((), ())),
            preferred_element_type=F32,
        ).astype(BF16)
        for d in range(1, 4):
            copy_m(k, d).start()

    for k, device in ((0, by_y), (1, by_x)):
        s = 2 * chips[2 - k] + core
        cols = slice(k * root, (k + 1) * root)
        copy_b(k, 0, by_x).wait_recv()
        root_part[s, :, cols] = (root_part[s, :, cols].astype(F32) + recv_b[k, 0].astype(F32)).astype(BF16)
        copy_c(k, device).start()

    coup_mass[0] = jnp.dot(full[0:order, :], part2[...], preferred_element_type=F32)
    coup_damp[0] = jnp.dot(full[order:2 * order, :], part2[...], preferred_element_type=F32)

    def copy_d(k, d):
        target = lax.rem(leaf + d, leaves)
        return pltpu.make_async_remote_copy(
            src_ref=root_strip.at[k, pl.ds(pl.multiple_of(target * out_rows, out_rows), out_rows), :],
            dst_ref=recv_d.at[k, d - 1],
            send_sem=ds_sem.at[k, d - 1],
            recv_sem=dr_sem.at[k, d - 1],
            device_id=(group, target),
            device_id_type=MESH,
        )

    for k in range(2):
        s = 2 * chips[3] + core
        cols = slice(k * root, (k + 1) * root)
        copy_b(k, 1, by_x).wait_recv()
        copy_c(k, by_x).wait_recv()
        root_strip[k] = (
            root_part[s, :, cols].astype(F32) + recv_b[k, 1].astype(F32) + recv_c[k].astype(F32)
        ).astype(BF16)
        for d in range(1, 4):
            copy_d(k, d).start()

    for k, out in ((0, modal_mass), (1, modal_damp)):
        total = modal_part[k, pl.ds(pl.multiple_of(leaf * modal_rows, modal_rows), modal_rows), :].astype(F32)
        for d in range(1, 4):
            copy_m(k, d).wait_recv()
            total = total + recv_m[k, d - 1].astype(F32)
        out[0] = total
    for k, out in ((0, root_mass), (1, root_damp)):
        total = root_strip[k, pl.ds(pl.multiple_of(leaf * out_rows, out_rows), out_rows), :].astype(F32)
        for d in range(1, 4):
            copy_d(k, d).wait_recv()
            total = total + recv_d[k, d - 1].astype(F32)
        out[...] = total

    for p in range(3):
        for way in range(2):
            for t in range(3):
                @pl.when(sends(way, t))
                def _():
                    hop(p, way, t).wait_send()
    for i in range(4):
        copy_a(i).wait_send()
    for k in range(2):
        copy_b(k, 0, by_x).wait_send()
        copy_b(k, 1, by_x).wait_send()
        copy_c(k, by_x).wait_send()
        for d in range(1, 4):
            copy_d(k, d).wait_send()
            copy_m(k, d).wait_send()


def fused_body(
    leaf_mass, leaf_damp, mass_coupling, damp_coupling, leaf_modes, interface_blocks, mid_modes, mid_constraint
):
    order = leaf_mass.shape[1]
    sep = leaf_modes.shape[2]
    shard, modes = mid_modes.shape[1:]
    root = mid_constraint.shape[2]
    leaves = lax.axis_size("leaf")
    groups = lax.axis_size("group")
    width = modes + root
    modal_rows = modes // leaves
    out_rows = root // (leaves * groups)
    strip = root // groups
    half = root // 2
    numbers = jnp.arange(interface_blocks.shape[1], dtype=jnp.int32)
    chosen = (interface_blocks[0][None, :] == numbers[:, None]).astype(F32)
    chosen = jnp.repeat(chosen, sep // interface_blocks.shape[1], axis=1)[:, None, :]
    anywhere = pl.BlockSpec(memory_space=pl.ANY)
    vmem = pl.BlockSpec(memory_space=pltpu.VMEM)
    dma = pltpu.SemaphoreType.DMA
    return pl.pallas_call(
        fused_kernel,
        out_shape=(
            jax.ShapeDtypeStruct((1, order, modes), F32),
            jax.ShapeDtypeStruct((1, order, modes), F32),
            jax.ShapeDtypeStruct((1, modal_rows, width), F32),
            jax.ShapeDtypeStruct((1, modal_rows, width), F32),
            jax.ShapeDtypeStruct((out_rows, root), F32),
            jax.ShapeDtypeStruct((out_rows, root), F32),
        ),
        in_specs=[anywhere] * 5 + [vmem] + [anywhere] * 2,
        out_specs=[vmem] * 6,
        scratch_shapes=[
            pltpu.VMEM((order, order), BF16),
            pltpu.VMEM((order, order), BF16),
            pltpu.VMEM((order, sep), BF16),
            pltpu.VMEM((order, sep), BF16),
            pltpu.VMEM((order, sep), BF16),
            pltpu.VMEM((sep, half), BF16),
            pltpu.VMEM((sep, half), BF16),
            pltpu.VMEM((sep, modes), BF16),
            pltpu.VMEM((3 * order, sep), BF16),
            pltpu.VMEM((2 * order, sep), BF16),
            pltpu.VMEM((3 * order, width), BF16),
            pltpu.VMEM((3 * order, width), BF16),
            pltpu.VMEM((groups, strip, 2 * root), BF16),
            pltpu.VMEM((4, strip, 2 * root), BF16),
            pltpu.VMEM((2, 2, strip, root), BF16),
            pltpu.VMEM((2, strip, root), BF16),
            pltpu.VMEM((2, strip, root), BF16),
            pltpu.VMEM((2, 3, out_rows, root), BF16),
            pltpu.VMEM((2, modes, width), BF16),
            pltpu.VMEM((2, 3, modal_rows, width), BF16),
            dma((5,)), dma((3,)), dma((3, 2, 3)), dma((3, 2, 3)),
            dma((4,)), dma((4,)), dma((2, 2)), dma((2, 2)), dma((2,)), dma((2,)),
            dma((2, 3)), dma((2, 3)), dma((2, 3)), dma((2, 3)),
        ],
        compiler_params=pltpu.CompilerParams(
            collective_id=0, has_side_effects=True, vmem_limit_bytes=56 * 1024 * 1024
        ),
    )(leaf_mass, leaf_damp, mass_coupling, damp_coupling, leaf_modes, chosen, mid_modes, mid_constraint)


def solution(mesh):
    fits = mesh.shape["group"] == 8 and mesh.shape["leaf"] == 4
    return jax.shard_map(
        fused_body if fits else body,
        mesh=mesh,
        in_specs=(
            P(("group", "leaf"), None, None),
            P(("group", "leaf"), None, None),
            P(("group", "leaf"), None, None),
            P(("group", "leaf"), None, None),
            P(("group", "leaf"), None, None),
            P(("group", "leaf"), None),
            P("group", "leaf", None),
            P("group", "leaf", None),
        ),
        out_specs=(
            P(("group", "leaf"), None, None),
            P(("group", "leaf"), None, None),
            P("group", "leaf", None),
            P("group", "leaf", None),
            P(("group", "leaf"), None),
            P(("group", "leaf"), None),
        ),
        check_vma=False,
    )
```

```python
import jax
import jax.numpy as jnp
from jax import lax
from jax.experimental import pallas as pl
from jax.experimental.pallas import tpu as pltpu
from jax.sharding import PartitionSpec as P


def to_middle(stacked, onehot, block_count, block_size):
    rows_total, width_total = stacked.shape
    moved = jnp.einsum(
        "lbk,bj->ljk",
        stacked.reshape(rows_total, block_count, block_size),
        onehot,
        preferred_element_type=jnp.float32,
    )
    return moved.astype(jnp.bfloat16).reshape(rows_total, width_total)


def left_product(first_operand, second_operand):
    return lax.dot_general(
        first_operand, second_operand, (((0,), (0,)), ((), ())), preferred_element_type=jnp.float32
    )


def body(
    leaf_mass,
    leaf_damp,
    mass_coupling,
    damp_coupling,
    leaf_modes,
    interface_blocks,
    mid_modes,
    mid_constraint,
):
    leaf_order = leaf_mass.shape[1]
    block_count = interface_blocks.shape[1]
    sep_width = leaf_modes.shape[2]
    block_size = sep_width // block_count
    mode_count = mid_modes.shape[2]
    root_width = mid_constraint.shape[2]
    basis_width = mode_count + root_width
    leaf_count = lax.axis_size("leaf")
    group_count = lax.axis_size("group")
    onehot = (
        interface_blocks[0][:, None] == jnp.arange(block_count, dtype=jnp.int32)[None, :]
    ).astype(jnp.bfloat16)
    placed = to_middle(
        jnp.concatenate([leaf_modes[0], mass_coupling[0], damp_coupling[0]], axis=0),
        onehot,
        block_count,
        block_size,
    )
    constraint = placed[:leaf_order]
    sides = placed[leaf_order:].astype(jnp.float32)
    product = jnp.dot(
        jnp.concatenate([leaf_mass[0], leaf_damp[0]], axis=0),
        constraint,
        preferred_element_type=jnp.float32,
    )
    half_work = (0.5 * product + sides).astype(jnp.bfloat16)
    full_work = (product + sides).astype(jnp.bfloat16)
    basis_rows = jnp.concatenate([mid_modes[0], mid_constraint[0]], axis=1)
    mode_basis = lax.all_gather(basis_rows, "leaf", axis=0, tiled=True)
    left_sum = jnp.dot(constraint, mode_basis, preferred_element_type=jnp.float32)
    right_sum = jnp.dot(half_work, mode_basis, preferred_element_type=jnp.float32)
    coupling = jnp.dot(full_work, mode_basis[:, :mode_count], preferred_element_type=jnp.float32)
    left_part = left_sum.astype(jnp.bfloat16)
    right_part = right_sum.astype(jnp.bfloat16)
    right_mass = right_part[:leaf_order]
    right_damp = right_part[leaf_order:]

    def projected_rows(first_row, amount, first_col):
        left_rows = lax.dynamic_slice_in_dim(left_part, first_row, amount, 1)
        right_rows = lax.dynamic_slice_in_dim(right_part, first_row, amount, 1)
        left_cols = left_part[:, first_col:]
        mass_term = left_product(left_rows, right_mass[:, first_col:]) + left_product(
            right_rows[:leaf_order], left_cols
        )
        damp_term = left_product(left_rows, right_damp[:, first_col:]) + left_product(
            right_rows[leaf_order:], left_cols
        )
        return jnp.concatenate([mass_term, damp_term], axis=1)

    modal_part = lax.psum_scatter(
        projected_rows(jnp.int32(0), mode_count // leaf_count * lax.axis_size("leaf"), 0),
        "leaf",
        scatter_dimension=0,
        tiled=True,
    )
    root_part = lax.psum_scatter(
        projected_rows(
            jnp.int32(0) + mode_count,
            root_width // (group_count * leaf_count) * lax.axis_size(("group", "leaf")),
            mode_count,
        ),
        ("group", "leaf"),
        scatter_dimension=0,
        tiled=True,
    )
    return (
        coupling[:leaf_order][None],
        coupling[leaf_order:][None],
        modal_part[:, :basis_width][None],
        modal_part[:, basis_width:][None],
        root_part[:, :root_width],
        root_part[:, root_width:],
    )


F32 = jnp.float32
BF16 = jnp.bfloat16
MESH = pl.DeviceIdType.MESH
STRIP = 128
TILE = 256


def fused_kernel(
    leaf_mass, leaf_damp, mass_side, damp_side, leaf_modes, blocks, mid_modes, mid_constraint,
    coup_mass, coup_damp, modal_mass, modal_damp, root_mass, root_damp,
    mass_v, damp_v, mside_v, dside_v, modes_v,
    part0, part1, part2, work, full, q_one, q_two,
    root_part, recv_a, recv_b, recv_c, root_strip, recv_d, modal_part, recv_m,
    in_sem, own_sem, gs_sem, gr_sem, as_sem, ar_sem, bs_sem, br_sem, cs_sem, cr_sem,
    ds_sem, dr_sem, ms_sem, mr_sem,
):
    group = lax.axis_index("group")
    leaf = lax.axis_index("leaf")
    leaves = lax.axis_size("leaf")
    core, col, row = lax.rem(group, 2), lax.rem(group // 2, 2), group // 4
    by_core = (group + 1 - 2 * core, leaf)
    by_x = (group + 2 - 4 * col, leaf)
    by_y = (group + 4 - 8 * row, leaf)
    order = mass_v.shape[0]
    modes = mid_modes.shape[2]
    root = mid_constraint.shape[2]
    shard = mid_modes.shape[1]
    half = root // 2
    strip_rows = root // 8
    out_rows = root_mass.shape[0]
    modal_rows = modal_mass.shape[1]
    width = modes + root
    others = [(group, lax.rem(leaf + d, leaves)) for d in range(1, 4)]

    inputs = [
        pltpu.make_async_copy(a.at[0], b, in_sem.at[i])
        for i, (a, b) in enumerate(
            ((leaf_mass, mass_v), (leaf_damp, damp_v), (mass_side, mside_v), (damp_side, dside_v), (leaf_modes, modes_v))
        )
    ]
    own_src = (mid_constraint.at[0, :, 0:half], mid_constraint.at[0, :, half:root], mid_modes.at[0])
    parts = (part0, part1, part2)

    def rows_of(index):
        return pl.ds(pl.multiple_of(index * shard, shard), shard)

    own = [
        pltpu.make_async_copy(own_src[p], parts[p].at[rows_of(leaf), :], own_sem.at[p]) for p in range(3)
    ]

    barrier = pltpu.get_barrier_semaphore()
    for dev in [by_core, by_x, by_y] + others:
        pl.semaphore_signal(barrier, inc=1, device_id=dev, device_id_type=MESH)
    for c in inputs:
        c.start()
    for c in own:
        c.start()
    pl.semaphore_wait(barrier, 6)

    def hop(p, way, t):
        index = leaf - t if way == 0 else leaf + t
        target = leaf + 1 if way == 0 else leaf - 1
        place = parts[p].at[rows_of(index), :]
        return pltpu.make_async_remote_copy(
            src_ref=own_src[p] if t == 0 else place,
            dst_ref=place,
            send_sem=gs_sem.at[p, way, t],
            recv_sem=gr_sem.at[p, way, t],
            device_id=(group, target),
            device_id_type=MESH,
        )

    def sends(way, t):
        if way == 0:
            return (leaf + 1 < leaves) & (leaf >= t)
        return (leaf >= 1) & (leaf + t < leaves)

    def start_hop(p, t):
        for way in range(2):
            @pl.when(sends(way, t))
            def _():
                hop(p, way, t).start()

    def arrive(p, t):
        for way in range(2):
            has = leaf >= t if way == 0 else leaf + t < leaves

            @pl.when(has)
            def _():
                index = leaf - t if way == 0 else leaf + t
                pltpu.make_async_remote_copy(
                    src_ref=parts[p].at[rows_of(index), :],
                    dst_ref=parts[p].at[rows_of(index), :],
                    send_sem=gs_sem.at[p, way, t],
                    recv_sem=gr_sem.at[p, way, t - 1],
                    device_id=(group, lax.rem(leaf + 1, leaves)),
                    device_id_type=MESH,
                ).wait_recv()
        if t < 3:
            start_hop(p, t)

    start_hop(0, 0)
    for c in inputs:
        c.wait()

    def form(pair):
        chosen = [blocks[2 * pair + i].astype(BF16) for i in range(2)]

        def moved(ref):
            sums = [None, None]
            for b in range(12):
                lanes = slice(128 * b, 128 * (b + 1))
                for i in range(2):
                    term = ref[:, lanes] * chosen[i][:, lanes]
                    sums[i] = term if b == 0 else sums[i] + term
            return jnp.concatenate(sums, axis=1)

        here = pl.ds(pl.multiple_of(pair * 256, 256), 256)
        constraint = moved(modes_v)
        work[order:2 * order, here] = constraint
        for k, (block, side) in enumerate(((mass_v, mside_v), (damp_v, dside_v))):
            product = jnp.dot(block[...], constraint, preferred_element_type=F32)
            side_part = moved(side).astype(F32)
            work[2 * order * k:2 * order * k + order, here] = (0.5 * product + side_part).astype(BF16)
            full[order * k:order * (k + 1), here] = (product + side_part).astype(BF16)

    def multiply(p, first, size, low=0, high=6):
        @pl.loop(low, high)
        def _(m):
            tile = work[pl.ds(pl.multiple_of(m * TILE, TILE), TILE), :]
            value = jnp.dot(tile, parts[p][...], preferred_element_type=F32).astype(BF16)
            other = 4 - 2 * (m // 2) + lax.rem(m, 2)
            q_one[pl.ds(pl.multiple_of(m * TILE, TILE), TILE), first:first + size] = value
            q_two[pl.ds(pl.multiple_of(other * TILE, TILE), TILE), first:first + size] = value

    def pairs_of(k):
        if k == 0:
            return q_two, q_one
        return q_one, q_two

    pl.loop(0, 3)(form)
    arrive(0, 1)
    start_hop(1, 0)
    pl.loop(3, 6)(form)
    arrive(0, 2)
    arrive(0, 3)
    own[0].wait()
    multiply(0, modes, half)
    arrive(1, 1)
    start_hop(2, 0)
    arrive(1, 2)
    arrive(1, 3)
    own[1].wait()
    multiply(1, modes + half, half, 0, 3)
    arrive(2, 1)
    multiply(1, modes + half, half, 3, 6)
    arrive(2, 2)

    def strip_value(s, k):
        turned, straight = pairs_of(k)
        columns = pl.ds(pl.multiple_of(modes + s * strip_rows, 128), strip_rows)
        lhs = turned[order:3 * order, columns]
        return lax.dot_general(
            lhs, straight[0:2 * order, modes:width], (((0,), (0,)), ((), ())), preferred_element_type=F32
        )

    def fill_strip(s):
        for k in range(2):
            root_part[s, :, k * root:(k + 1) * root] = strip_value(s, k).astype(BF16)

    chips = (
        2 * (1 - row) + 1 - col,
        2 * row + 1 - col,
        2 * (1 - row) + col,
        2 * row + col,
    )

    def copy_a(i):
        return pltpu.make_async_remote_copy(
            src_ref=root_part.at[2 * chips[i] + 1 - core],
            dst_ref=recv_a.at[i],
            send_sem=as_sem.at[i],
            recv_sem=ar_sem.at[i],
            device_id=by_core,
            device_id_type=MESH,
        )

    def copy_b(k, slot, device):
        chip = chips[0] if slot == 0 else chips[1 + k]
        return pltpu.make_async_remote_copy(
            src_ref=root_part.at[2 * chip + core, :, k * root:(k + 1) * root],
            dst_ref=recv_b.at[k, slot],
            send_sem=bs_sem.at[k, slot],
            recv_sem=br_sem.at[k, slot],
            device_id=device,
            device_id_type=MESH,
        )

    def copy_c(k, device):
        chip = chips[2 - k]
        return pltpu.make_async_remote_copy(
            src_ref=root_part.at[2 * chip + core, :, k * root:(k + 1) * root],
            dst_ref=recv_c.at[k],
            send_sem=cs_sem.at[k],
            recv_sem=cr_sem.at[k],
            device_id=device,
            device_id_type=MESH,
        )

    for i in range(4):
        fill_strip(2 * chips[i] + 1 - core)
        copy_a(i).start()
    own[2].wait()
    arrive(2, 3)
    multiply(2, 0, modes)

    def modal_place(way, r):
        index = 3 - r + leaf if way == 0 else r - 3 + leaf
        return pl.ds(pl.multiple_of(index * modal_rows, modal_rows), modal_rows)

    def copy_m(k, way, r):
        return pltpu.make_async_remote_copy(
            src_ref=modal_part.at[k, modal_place(way, r), :],
            dst_ref=recv_m.at[k, way, r],
            send_sem=ms_sem.at[k, way, r],
            recv_sem=mr_sem.at[k, way, r],
            device_id=(group, leaf + 1 if way == 0 else leaf - 1),
            device_id_type=MESH,
        )

    def came_m(k, way, r):
        return pltpu.make_async_remote_copy(
            src_ref=recv_m.at[k, way, r],
            dst_ref=recv_m.at[k, way, r],
            send_sem=ms_sem.at[k, way, r],
            recv_sem=mr_sem.at[k, way, r],
            device_id=(group, lax.rem(leaf + 1, leaves)),
            device_id_type=MESH,
        )

    def modal_step(r):
        for k in range(2):
            for way in range(2):
                depth = leaf if way == 0 else leaves - 1 - leaf
                if r > 0:
                    @pl.when((depth >= 1) & (depth <= r))
                    def _():
                        came_m(k, way, r - 1).wait_recv()
                        at = modal_place(way, r)
                        modal_part[k, at, :] = (
                            modal_part[k, at, :].astype(F32) + recv_m[k, way, r - 1].astype(F32)
                        ).astype(BF16)

                    @pl.when(depth <= r - 1)
                    def _():
                        copy_m(k, way, r - 1).wait_send()

                @pl.when(depth <= r)
                def _():
                    copy_m(k, way, r).start()

    for k in range(2):
        turned, straight = pairs_of(k)
        modal_part[k] = lax.dot_general(
            turned[order:3 * order, 0:modes], straight[0:2 * order, :], (((0,), (0,)), ((), ())),
            preferred_element_type=F32,
        ).astype(BF16)
        for way in range(2):
            depth = leaf if way == 0 else leaves - 1 - leaf

            @pl.when(depth == 0)
            def _():
                copy_m(k, way, 0).start()

    for i in range(4):
        s = 2 * chips[i] + core
        fill_strip(s)
        copy_a(i).wait_recv()
        root_part[s] = (root_part[s].astype(F32) + recv_a[i].astype(F32)).astype(BF16)
        if i == 0:
            copy_b(0, 0, by_x).start()
            copy_b(1, 0, by_y).start()
        if i == 1:
            copy_b(0, 1, by_x).start()
        if i == 2:
            copy_b(1, 1, by_y).start()
    modal_step(1)
    coup_mass[0] = jnp.dot(full[0:order, :], part2[...], preferred_element_type=F32)
    coup_damp[0] = jnp.dot(full[order:2 * order, :], part2[...], preferred_element_type=F32)

    for k, device in ((0, by_y), (1, by_x)):
        s = 2 * chips[2 - k] + core
        cols = slice(k * root, (k + 1) * root)
        copy_b(k, 0, by_x).wait_recv()
        root_part[s, :, cols] = (root_part[s, :, cols].astype(F32) + recv_b[k, 0].astype(F32)).astype(BF16)
        copy_c(k, device).start()

    modal_step(2)

    def copy_d(k, d):
        target = lax.rem(leaf + d, leaves)
        return pltpu.make_async_remote_copy(
            src_ref=root_strip.at[k, pl.ds(pl.multiple_of(target * out_rows, out_rows), out_rows), :],
            dst_ref=recv_d.at[k, d - 1],
            send_sem=ds_sem.at[k, d - 1],
            recv_sem=dr_sem.at[k, d - 1],
            device_id=(group, target),
            device_id_type=MESH,
        )

    for k in range(2):
        s = 2 * chips[3] + core
        cols = slice(k * root, (k + 1) * root)
        copy_b(k, 1, by_x).wait_recv()
        copy_c(k, by_x).wait_recv()
        root_strip[k] = (
            root_part[s, :, cols].astype(F32) + recv_b[k, 1].astype(F32) + recv_c[k].astype(F32)
        ).astype(BF16)
        for d in range(1, 4):
            copy_d(k, d).start()

    for k, out in ((0, modal_mass), (1, modal_damp)):
        out[0] = modal_part[k, pl.ds(pl.multiple_of(leaf * modal_rows, modal_rows), modal_rows), :].astype(F32)
        for way in range(2):
            depth = leaf if way == 0 else leaves - 1 - leaf

            @pl.when(depth >= 1)
            def _():
                came_m(k, way, 2).wait_recv()
                out[0] = out[0] + recv_m[k, way, 2].astype(F32)

            @pl.when(depth <= 2)
            def _():
                copy_m(k, way, 2).wait_send()
    for k, out in ((0, root_mass), (1, root_damp)):
        total = root_strip[k, pl.ds(pl.multiple_of(leaf * out_rows, out_rows), out_rows), :].astype(F32)
        for d in range(1, 4):
            copy_d(k, d).wait_recv()
            total = total + recv_d[k, d - 1].astype(F32)
        out[...] = total

    for p in range(3):
        for way in range(2):
            for t in range(3):
                @pl.when(sends(way, t))
                def _():
                    hop(p, way, t).wait_send()
    for i in range(4):
        copy_a(i).wait_send()
    for k in range(2):
        copy_b(k, 0, by_x).wait_send()
        copy_b(k, 1, by_x).wait_send()
        copy_c(k, by_x).wait_send()
        for d in range(1, 4):
            copy_d(k, d).wait_send()


def hand_over(*refs):
    sem = refs[12]
    copies = [pltpu.make_async_copy(refs[i], refs[6 + i], sem.at[i]) for i in range(6)]
    for c in copies:
        c.start()
    for c in copies:
        c.wait()


def fused_body(
    leaf_mass, leaf_damp, mass_coupling, damp_coupling, leaf_modes, interface_blocks, mid_modes, mid_constraint
):
    order = leaf_mass.shape[1]
    sep = leaf_modes.shape[2]
    shard, modes = mid_modes.shape[1:]
    root = mid_constraint.shape[2]
    leaves = lax.axis_size("leaf")
    groups = lax.axis_size("group")
    width = modes + root
    modal_rows = modes // leaves
    out_rows = root // (leaves * groups)
    strip = root // groups
    half = root // 2
    numbers = jnp.arange(interface_blocks.shape[1], dtype=jnp.int32)
    chosen = (interface_blocks[0][None, :] == numbers[:, None]).astype(F32)
    chosen = jnp.repeat(chosen, sep // interface_blocks.shape[1], axis=1)[:, None, :]
    anywhere = pl.BlockSpec(memory_space=pl.ANY)
    vmem = pl.BlockSpec(memory_space=pltpu.VMEM)
    dma = pltpu.SemaphoreType.DMA
    shapes = (
        jax.ShapeDtypeStruct((1, order, modes), F32),
        jax.ShapeDtypeStruct((1, order, modes), F32),
        jax.ShapeDtypeStruct((1, modal_rows, width), F32),
        jax.ShapeDtypeStruct((1, modal_rows, width), F32),
        jax.ShapeDtypeStruct((out_rows, root), F32),
        jax.ShapeDtypeStruct((out_rows, root), F32),
    )
    results = pl.pallas_call(
        fused_kernel,
        out_shape=shapes,
        in_specs=[anywhere] * 5 + [vmem] + [anywhere] * 2,
        out_specs=[vmem] * 6,
        scratch_shapes=[
            pltpu.VMEM((order, order), BF16),
            pltpu.VMEM((order, order), BF16),
            pltpu.VMEM((order, sep), BF16),
            pltpu.VMEM((order, sep), BF16),
            pltpu.VMEM((order, sep), BF16),
            pltpu.VMEM((sep, half), BF16),
            pltpu.VMEM((sep, half), BF16),
            pltpu.VMEM((sep, modes), BF16),
            pltpu.VMEM((3 * order, sep), BF16),
            pltpu.VMEM((2 * order, sep), BF16),
            pltpu.VMEM((3 * order, width), BF16),
            pltpu.VMEM((3 * order, width), BF16),
            pltpu.VMEM((groups, strip, 2 * root), BF16),
            pltpu.VMEM((4, strip, 2 * root), BF16),
            pltpu.VMEM((2, 2, strip, root), BF16),
            pltpu.VMEM((2, strip, root), BF16),
            pltpu.VMEM((2, strip, root), BF16),
            pltpu.VMEM((2, 3, out_rows, root), BF16),
            pltpu.VMEM((2, modes, width), BF16),
            pltpu.VMEM((2, 2, 3, modal_rows, width), BF16),
            dma((5,)), dma((3,)), dma((3, 2, 3)), dma((3, 2, 3)),
            dma((4,)), dma((4,)), dma((2, 2)), dma((2, 2)), dma((2,)), dma((2,)),
            dma((2, 3)), dma((2, 3)), dma((2, 2, 3)), dma((2, 2, 3)),
        ],
        compiler_params=pltpu.CompilerParams(
            collective_id=0, has_side_effects=True, vmem_limit_bytes=56 * 1024 * 1024
        ),
    )(leaf_mass, leaf_damp, mass_coupling, damp_coupling, leaf_modes, chosen, mid_modes, mid_constraint)
    return pl.pallas_call(
        hand_over,
        out_shape=shapes,
        in_specs=[anywhere] * 6,
        out_specs=[anywhere] * 6,
        scratch_shapes=[dma((6,))],
    )(*results)


def solution(mesh):
    fits = mesh.shape["group"] == 8 and mesh.shape["leaf"] == 4
    return jax.shard_map(
        fused_body if fits else body,
        mesh=mesh,
        in_specs=(
            P(("group", "leaf"), None, None),
            P(("group", "leaf"), None, None),
            P(("group", "leaf"), None, None),
            P(("group", "leaf"), None, None),
            P(("group", "leaf"), None, None),
            P(("group", "leaf"), None),
            P("group", "leaf", None),
            P("group", "leaf", None),
        ),
        out_specs=(
            P(("group", "leaf"), None, None),
            P(("group", "leaf"), None, None),
            P("group", "leaf", None),
            P("group", "leaf", None),
            P(("group", "leaf"), None),
            P(("group", "leaf"), None),
        ),
        check_vma=False,
    )
```
